32 devices in a mesh: seq: 16 (over z, x, core), dp: 2 (over y).
Axes of the slice: x: 2, y: 2, z: 4, core: 2. Of those that a mesh axis runs over, the one named last changes fastest.
Arguments:
- query_in: bfloat16 [4096, 2048], P('seq', 'dp'), may hold values from -6 to 6
- key_in: bfloat16 [4096, 2048], P('seq', 'dp'), may hold values from -6 to 6
- value_in: bfloat16 [4096, 2048], P('seq', 'dp'), may hold values from -6 to 6
- filters: bfloat16 [16, 2048], P(None, 'dp'), may hold values from -0.125 to 0.125
- out_weight: bfloat16 [2048, 2048], P('dp'), may hold values from -0.125 to 0.125
- grad_mixed: bfloat16 [4096, 2048], P('seq', 'dp'), may hold values from -6 to 6
Outputs:
- grad_query: bfloat16 [4096, 2048], P('seq', 'dp')
- grad_key: bfloat16 [4096, 2048], P('seq', 'dp')
- grad_value: bfloat16 [4096, 2048], P('seq', 'dp')
- grad_weight: float32 [2048, 2048], P('dp', 'seq')
- grad_filters: float32 [16, 2048], P('dp', 'seq')
The draws below stay inside these ranges and needn't reach their ends.
All inputs are finite; a program needn't handle non-finite values.
Results may differ from the reference program's by a relative error of at most 0.0049.
Values may be sent and summed in bfloat16 or wider, within the bound.
A program may use at most 128 MiB of HBM per device.

```python
import jax
import jax.numpy as jnp
from jax import lax

CHANNELS = 2048
NUM_FILTERS = 16
FILTER_LEN = 2048
TOKENS = 4096


def spiked(array, stream_key, source, target, shards_of, factor):
    owner, partner = [(jnp.arange(array.shape[dim]) // (array.shape[dim] // shards_of)).reshape([-1 if axis == dim else 1 for axis in range(array.ndim)]) for dim in (source, target)]
    chosen = jax.random.permutation(stream_key, shards_of)[partner]
    strong = (owner == chosen) | (owner == (partner + shards_of // 2) % shards_of)
    return jnp.where(strong, factor * array, array)


def steps_of(stream_key, shape, shards, least, high):
    gain, own = 1.0, jax.random.fold_in(stream_key, 6)
    for axis_at, blocks in shards:
        heights = jnp.exp(jax.random.uniform(jax.random.fold_in(own, axis_at), (blocks,), jnp.float32, least / len(shards), high / len(shards)))
        gain = gain * jnp.repeat(heights, shape[axis_at] // blocks).reshape([-1 if axis == axis_at else 1 for axis in range(len(shape))])
    return gain


def gaussian(key, dims, width, limit, shards=(), dtype=jnp.bfloat16):
    gain = steps_of(key, dims, shards, -0.22, 0.18) if shards else 1.0
    result = jax.random.normal(key, dims, jnp.float32) * width * gain
    return jnp.minimum(jnp.maximum(result, -limit), limit).astype(dtype)


def noise_with(stream_key, shape, spread, reach, pieces, heavy, held_as=jnp.bfloat16):
    values = spread * jax.random.normal(stream_key, shape, jnp.float32)
    if pieces:
        values = values * steps_of(stream_key, shape, pieces, -0.22, 0.18)
    return jnp.clip(spiked(values, jax.random.fold_in(stream_key, 3), *heavy), -reach, reach).astype(held_as)


def setup_inputs(seed: int = 0) -> dict:
    streams_of = jax.random.split(jax.random.key(seed), 7)
    return {
        "query_in": gaussian(streams_of[0], (TOKENS, CHANNELS), 1.0, 6.0, ((0, 16), (1, 2))),
        "key_in": gaussian(streams_of[1], (TOKENS, CHANNELS), 1.0, 6.0, ((0, 16), (1, 2))),
        "value_in": gaussian(streams_of[2], (TOKENS, CHANNELS), 1.0, 6.0, ((0, 16), (1, 2))),
        "filters": gaussian(streams_of[3], (NUM_FILTERS, FILTER_LEN), FILTER_LEN ** -0.5, 0.125, ((1, 2),)),
        "out_weight": gaussian(streams_of[4], (CHANNELS, CHANNELS), CHANNELS ** -0.5, 0.125, ((0, 2),)),
        "grad_mixed": noise_with(streams_of[5], (TOKENS, CHANNELS), 1.0, 6.0, ((0, 16), (1, 2)), (0, 1, 16, 2.0)),
    }


def causal_filter(signal, taps_row):
    length = signal.shape[0]
    period = length + taps_row.shape[0]
    spectrum = jnp.fft.rfft(signal, n=period, axis=0) * jnp.fft.rfft(taps_row, n=period)[:, None]
    return jnp.fft.irfft(spectrum, n=period, axis=0)[:length]


def lag_products(grads, inputs):
    length = grads.shape[0]
    period = length + FILTER_LEN
    spectrum = jnp.conj(jnp.fft.rfft(inputs, n=period, axis=0)) * jnp.fft.rfft(grads, n=period, axis=0)
    return jnp.sum(jnp.fft.irfft(spectrum, n=period, axis=0)[:FILTER_LEN], axis=1)


def reference(query_in, key_in, value_in, filters, out_weight, grad_mixed):
    group_width = CHANNELS // NUM_FILTERS
    products = (key_in.astype(jnp.float32) * value_in.astype(jnp.float32)).astype(jnp.bfloat16)
    taps_all = filters.astype(jnp.float32)

    def by_group(tensor):
        return tensor.astype(jnp.float32).reshape(TOKENS, NUM_FILTERS, group_width).transpose(1, 0, 2)

    def back_layout(tensor):
        return tensor.transpose(1, 0, 2).reshape(TOKENS, CHANNELS)

    def forward_group(member):
        return causal_filter(member[0], member[1])

    def backward_group(member):
        return causal_filter(member[0][::-1], member[1])[::-1]

    def filter_group(member):
        return lag_products(member[0], member[1])

    conv_out = back_layout(lax.map(forward_group, (by_group(products), taps_all)))
    gated = (query_in.astype(jnp.float32) * conv_out).astype(jnp.bfloat16)
    grad_gated = jnp.dot(grad_mixed, out_weight.T, preferred_element_type=jnp.float32)
    grad_query = (grad_gated * conv_out).astype(jnp.bfloat16)
    grad_conv = (grad_gated * query_in.astype(jnp.float32)).astype(jnp.bfloat16)
    grad_products = back_layout(lax.map(backward_group, (by_group(grad_conv), taps_all)))
    grad_key = (grad_products * value_in.astype(jnp.float32)).astype(jnp.bfloat16)
    grad_value = (grad_products * key_in.astype(jnp.float32)).astype(jnp.bfloat16)
    grad_filters = lax.map(filter_group, (by_group(grad_conv), by_group(products)))
    grad_weight = jnp.dot(gated.T, grad_mixed, preferred_element_type=jnp.float32)
    return (grad_query, grad_key, grad_value, grad_weight, grad_filters)
```

```python
import jax
import jax.numpy as jnp
from jax import lax
from jax.experimental import pallas as pl
from jax.experimental.pallas import tpu as pltpu
from jax.sharding import PartitionSpec as P

NUM_FILTERS = 16


def from_behind(block, axis, distance):
    devices = range(lax.axis_size(axis))
    route = [(i - distance, i) for i in devices if i - distance in devices]
    return lax.ppermute(block, axis, route)


def band_matrix(vector, row_count, col_count):
    period = vector.shape[0]
    tiled = jnp.tile(vector, (row_count,))[: row_count * (period - 1)]
    return tiled.reshape(row_count, period - 1)[:, :col_count]


def input_doubling(own_shard, reach_count):
    window = own_shard
    covered = 1
    for bit_index in range(reach_count.bit_length() - 1):
        window = jnp.concatenate([from_behind(window, "seq", covered), window], 0)
        covered = covered * 2
    farthest = from_behind(own_shard, "seq", reach_count)
    return jnp.concatenate([farthest, window], 0)


def grad_doubling(own_shard, reach_count):
    window = own_shard
    covered = 1
    for bit_index in range(reach_count.bit_length() - 1):
        window = jnp.concatenate([window, from_behind(window, "seq", -covered)], 0)
        covered = covered * 2
    farthest = from_behind(own_shard, "seq", -reach_count)
    return jnp.concatenate([window, farthest], 0)


def per_device(query_in, key_in, value_in, filters, out_weight, grad_mixed):
    tok_rows, local_width = query_in.shape
    dp_count = lax.axis_size("dp")
    filter_len = filters.shape[1] * dp_count
    local_filters = NUM_FILTERS // dp_count
    group_width = local_width // local_filters
    reach_count = filter_len // tok_rows
    span_rows = filter_len + tok_rows
    period = span_rows + tok_rows
    all_taps = lax.all_gather(filters, "dp", axis=1, tiled=True)
    owned_taps = lax.dynamic_slice_in_dim(
        all_taps, lax.axis_index("dp") * local_filters, local_filters, 0
    )
    products = (key_in.astype(jnp.float32) * value_in.astype(jnp.float32)).astype(jnp.bfloat16)
    window_in = input_doubling(products, reach_count)
    head_zeros = jnp.zeros((local_filters, 1), jnp.bfloat16)
    tail_zeros = jnp.zeros((local_filters, period - 1 - filter_len), jnp.bfloat16)
    forward_vectors = jnp.concatenate([head_zeros, owned_taps[:, ::-1], tail_zeros], 1)
    after_zeros = jnp.zeros((local_filters, period - filter_len), jnp.bfloat16)
    backward_vectors = jnp.concatenate([owned_taps, after_zeros], 1)
    conv_parts = []
    for group_index in range(local_filters):
        forward_band = band_matrix(forward_vectors[group_index], tok_rows, span_rows)
        window_part = window_in[:, group_index * group_width : (group_index + 1) * group_width]
        conv_parts.append(jnp.dot(forward_band, window_part, preferred_element_type=jnp.float32))
    conv_out = jnp.concatenate(conv_parts, 1)
    gated = (query_in.astype(jnp.float32) * conv_out).astype(jnp.bfloat16)
    block_in = lax.all_gather(grad_mixed, "dp", axis=1, tiled=True)
    grad_part = lax.dot_general(
        block_in, out_weight, (((1,), (1,)), ((), ())), preferred_element_type=jnp.float32
    )
    block_grad = lax.dot_general(
        gated, block_in, (((0,), (0,)), ((), ())), preferred_element_type=jnp.float32
    )
    grad_query = (grad_part * conv_out).astype(jnp.bfloat16)
    grad_conv = (grad_part * query_in.astype(jnp.float32)).astype(jnp.bfloat16)
    window_grad = grad_doubling(grad_conv, reach_count)
    grad_parts = []
    filter_rows = []
    for group_index in range(local_filters):
        low_col = group_index * group_width
        backward_band = band_matrix(backward_vectors[group_index], tok_rows, span_rows)
        grad_window = window_grad[:, low_col : low_col + group_width]
        grad_parts.append(jnp.dot(backward_band, grad_window, preferred_element_type=jnp.float32))
        own_grads = grad_conv[:, low_col : low_col + group_width]
        window_part = window_in[:, low_col : low_col + group_width]
        lagged = lax.dot_general(
            own_grads, window_part, (((1,), (1,)), ((), ())), preferred_element_type=jnp.float32
        )
        flattened = jnp.pad(lagged.reshape(tok_rows * span_rows), (0, tok_rows))
        skewed = flattened.reshape(tok_rows, span_rows + 1)
        diagonal_sums = jnp.sum(skewed, axis=0)
        filter_rows.append(diagonal_sums[1 : filter_len + 1][::-1])
    grad_products = jnp.concatenate(grad_parts, 1)
    grad_key = (grad_products * value_in.astype(jnp.float32)).astype(jnp.bfloat16)
    grad_value = (grad_products * key_in.astype(jnp.float32)).astype(jnp.bfloat16)
    filter_grad = jnp.stack(filter_rows, 0)
    grad_weight, grad_filters = (
        lax.psum_scatter(block_grad, "seq", scatter_dimension=1, tiled=True),
        lax.psum_scatter(filter_grad, "seq", scatter_dimension=1, tiled=True),
    )
    return (grad_query, grad_key, grad_value, grad_weight, grad_filters)


LEVEL = 4


def transposed(block):
    return block.astype(jnp.float32).T.astype(jnp.bfloat16)


def fused_kernel(
    query_ref, key_ref, value_ref, taps_ref, weight_ref, mixed_ref,
    gquery_ref, gkey_ref, gvalue_ref, gweight_ref, gfilters_ref,
    taps_all, mixed_all, weight_own, prod_out, prod_win, grad_win, query_lvl, gated_lvl,
    part_lvl, band_back, band_fwd, lags, gq_out, gq_in, gp_out, gp_in,
    gw_out, gw_in, gf_out, gf_in,
    weight_sem, taps_sem, prod_sem, query_sem, mixed_sem, xz_send, xz_recv, gz_send, gz_recv,
    gq_sem, gp_sem, gw_send, gw_recv, gf_send, gf_recv,
):
    f32, bf16 = jnp.float32, jnp.bfloat16
    seq_count = lax.axis_size("seq")
    me, dp_me = lax.axis_index("seq"), lax.axis_index("dp")
    level_count = seq_count // LEVEL
    level, rank = me // LEVEL, lax.rem(me, LEVEL)
    base = level * LEVEL
    rows, width = query_ref.shape
    chan = width // LEVEL
    group_filters = band_back.shape[0]
    group_width = chan // group_filters
    span = band_back.shape[2]
    blocks = span // rows
    reach = (blocks - 1) // LEVEL
    local_filters = group_filters * LEVEL
    piece = gweight_ref.shape[1]
    tap_piece = gfilters_ref.shape[1]

    def flip(index, offset):
        low, high = lax.rem(index, 2), index // 2
        if offset & 1:
            low = 1 - low
        if offset & 2:
            high = 1 - high
        return high * 2 + low

    peers = [flip(rank, offset) for offset in range(LEVEL)]
    ids = [(base + peer, dp_me) for peer in peers]
    across = (me, 1 - dp_me)

    def remote(src, dst, send, recv, device):
        return pltpu.make_async_remote_copy(
            src_ref=src, dst_ref=dst, send_sem=send, recv_sem=recv, device_id=device,
            device_id_type=pl.DeviceIdType.MESH)

    barrier = pltpu.get_barrier_semaphore()
    for step in range(1, seq_count):
        pl.semaphore_signal(barrier, inc=1, device_id=(lax.rem(me + step, seq_count), dp_me),
                            device_id_type=pl.DeviceIdType.MESH)
    pl.semaphore_signal(barrier, inc=1, device_id=across, device_id_type=pl.DeviceIdType.MESH)

    weight_copy = pltpu.make_async_copy(
        weight_ref.at[pl.ds(pl.multiple_of(rank * chan, chan), chan), :], weight_own, weight_sem)
    weight_copy.start()
    for part in range(LEVEL):
        cols = slice(part * chan, (part + 1) * chan)
        prod_out[part] = (key_ref[:, cols].astype(f32) * value_ref[:, cols].astype(f32)).astype(bf16)
    own_slot = reach * LEVEL

    def token_rows(part):
        return pl.ds(pl.multiple_of(part * rows, rows), rows)

    def chan_cols(part):
        return pl.ds(pl.multiple_of(part * chan, chan), chan)

    pl.semaphore_wait(barrier, seq_count)

    taps_copy = remote(taps_ref, taps_all.at[dp_me], taps_sem.at[0], taps_sem.at[1], across)
    taps_copy.start()
    prod_copies, query_copies = [], []
    for offset in range(1, LEVEL):
        copy = remote(prod_out.at[peers[offset]], prod_win.at[own_slot + rank],
                      prod_sem.at[0, offset], prod_sem.at[1, offset], ids[offset])
        copy.start()
        prod_copies.append(copy)

    def mixed_copy(sem, src, dp_at, part, device):
        dst = mixed_all.at[dp_at, token_rows(part), :]
        return remote(dst if src is None else src, dst, mixed_sem.at[0, sem], mixed_sem.at[1, sem], device)

    mixed_copies = [
        mixed_copy(0, mixed_ref, dp_me, rank, ids[2]),
        mixed_copy(1, mixed_ref, dp_me, rank, across),
        mixed_copy(2, mixed_ref, dp_me, rank, ids[1]),
    ]
    for copy in mixed_copies:
        copy.start()
    for offset in range(1, LEVEL):
        copy = remote(query_ref.at[:, chan_cols(peers[offset])], query_lvl.at[rank],
                      query_sem.at[0, offset], query_sem.at[1, offset], ids[offset])
        copy.start()
        query_copies.append(copy)

    prod_win[own_slot + rank] = prod_out[rank]
    query_lvl[rank] = query_ref[:, chan_cols(rank)]
    mixed_all[dp_me, token_rows(rank), :] = mixed_ref[...]
    taps_all[dp_me] = taps_ref[...]

    for hop in range(reach):
        @pl.when(level <= hop)
        def _():
            for part in range(LEVEL):
                prod_win[(reach - 1 - hop) * LEVEL + part] = jnp.zeros((rows, chan), bf16)

        @pl.when(level + hop + 1 >= level_count)
        def _():
            for part in range(LEVEL):
                grad_win[(hop + 1) * LEVEL + part] = jnp.zeros((rows, chan), bf16)

    def prod_hop(hop, offset):
        part = peers[offset]
        return remote(prod_win.at[(reach - hop) * LEVEL + part], prod_win.at[(reach - hop - 1) * LEVEL + part],
                      xz_send.at[hop, offset], xz_recv.at[hop, offset],
                      (lax.rem(me + LEVEL, seq_count), dp_me))

    def grad_hop(hop, offset):
        part = peers[offset]
        return remote(grad_win.at[hop * LEVEL + part], grad_win.at[(hop + 1) * LEVEL + part],
                      gz_send.at[hop, offset], gz_recv.at[hop, offset],
                      (lax.rem(me + seq_count - LEVEL, seq_count), dp_me))

    def prod_sends(hop):
        return (level >= hop) & (level < level_count - 1)

    def prod_takes(hop):
        return level >= hop + 1

    def grad_sends(hop):
        return (level + hop < level_count) & (level > 0)

    def grad_takes(hop):
        return level + hop + 1 < level_count

    for offset in range(LEVEL):
        if offset:
            wait_in = remote(prod_out.at[peers[offset]], prod_win.at[own_slot + peers[offset]],
                             prod_sem.at[0, offset], prod_sem.at[1, offset], ids[offset])
            wait_in.wait_recv()

        @pl.when(prod_sends(0))
        def _():
            prod_hop(0, offset).start()

    remote(taps_ref, taps_all.at[1 - dp_me], taps_sem.at[0], taps_sem.at[1], across).wait_recv()
    halves = taps_all.shape[0]
    row_at = lax.broadcasted_iota(jnp.int32, taps_all.shape[1:], 0)
    sub_at = lax.broadcasted_iota(jnp.int32, (8, span + rows), 0)
    for filt in range(group_filters):
        wanted = dp_me * local_filters + rank * group_filters + filt
        taps_row = jnp.concatenate(
            [jnp.sum(jnp.where(row_at == wanted, taps_all[half].astype(f32), 0.0), axis=0, keepdims=True)
             for half in range(halves)] + [jnp.zeros((1, 2 * rows), f32)], 1)
        band = jnp.broadcast_to(taps_row, (8, span + rows))
        for bit in (1, 2, 4):
            band = jnp.where((sub_at & bit) != 0, pltpu.roll(band, bit, 1), band)
        height = 8
        while height < rows:
            band = jnp.concatenate([band, pltpu.roll(band, height, 1)], 0)
            height *= 2
        for lag in range(blocks):
            tile = band[:, lag * rows : (lag + 1) * rows]
            band_back[filt, :, lag * rows : (lag + 1) * rows] = tile.astype(bf16)
            at = (blocks - 1 - lag) * rows
            band_fwd[filt, :, at : at + rows] = tile.T.astype(bf16)

    def mixed_wait(sem, dp_at, part):
        mixed_copy(sem, None, dp_at, part, across).wait_recv()

    mixed_wait(1, 1 - dp_me, rank)
    relay = mixed_copy(3, None, 1 - dp_me, rank, ids[1])
    relay.start()
    mixed_copies.append(relay)
    mixed_wait(0, dp_me, peers[2])
    for sem, device in ((4, across), (5, ids[1])):
        relay = mixed_copy(sem, None, dp_me, peers[2], device)
        relay.start()
        mixed_copies.append(relay)
    mixed_wait(2, dp_me, peers[1])
    mixed_wait(3, 1 - dp_me, peers[1])
    mixed_wait(5, dp_me, peers[3])
    weight_copy.wait()

    def level_grad(offset):
        part = peers[offset]
        total = jnp.zeros((rows, chan), f32)
        for half in range(halves):
            total += lax.dot_general(
                mixed_all[half, token_rows(part), :], weight_own[:, half * width : (half + 1) * width],
                (((1,), (1,)), ((), ())), preferred_element_type=f32)
        part_lvl[part] = total
        if offset:
            remote(query_ref.at[:, chan_cols(peers[offset])], query_lvl.at[part],
                   query_sem.at[0, offset], query_sem.at[1, offset], ids[offset]).wait_recv()
        grad_win[part] = (total * query_lvl[part].astype(f32)).astype(bf16)

        @pl.when(grad_sends(0))
        def _():
            grad_hop(0, offset).start()

    level_grad(0)
    level_grad(1)
    for hop in range(1, reach):
        for offset in range(LEVEL):
            @pl.when(prod_takes(hop - 1))
            def _():
                prod_hop(hop - 1, offset).wait_recv()

            @pl.when(prod_sends(hop))
            def _():
                prod_hop(hop, offset).start()
    mixed_wait(4, 1 - dp_me, peers[2])
    relay = mixed_copy(6, None, 1 - dp_me, peers[2], ids[1])
    relay.start()
    mixed_copies.append(relay)
    level_grad(2)
    mixed_wait(6, 1 - dp_me, peers[3])
    level_grad(3)

    for offset in range(LEVEL):
        @pl.when(prod_takes(reach - 1))
        def _():
            prod_hop(reach - 1, offset).wait_recv()

    def filt_cols(filt):
        return slice(filt * group_width, (filt + 1) * group_width)

    gq_copies, gp_copies = [], []
    for offset in (1, 2, 3, 0):
        part = peers[offset]
        conv = jnp.concatenate(
            [jnp.dot(band_fwd[filt],
                     prod_win[pl.ds(part, blocks), :, filt_cols(filt)].reshape(span, group_width),
                     preferred_element_type=f32) for filt in range(group_filters)], 1)
        gated = (query_lvl[part].astype(f32) * conv).astype(bf16)
        gated_lvl[:, token_rows(part)] = transposed(gated)
        grad = (part_lvl[part] * conv).astype(bf16)
        if offset:
            gq_out[part] = grad
            copy = remote(gq_out.at[part], gq_in.at[rank], gq_sem.at[0, offset], gq_sem.at[1, offset], ids[offset])
            copy.start()
            gq_copies.append(copy)
        else:
            gq_in[part] = grad

    for hop in range(1, reach):
        for offset in range(LEVEL):
            @pl.when(grad_takes(hop - 1))
            def _():
                grad_hop(hop - 1, offset).wait_recv()

            @pl.when(grad_sends(hop))
            def _():
                grad_hop(hop, offset).start()

    per_half = width // piece

    def weight_piece(dest):
        cols = pl.ds(pl.multiple_of(lax.rem(dest, per_half) * piece, piece), piece)
        return jnp.dot(gated_lvl[...], mixed_all[dest // per_half, :, cols],
                       preferred_element_type=f32).astype(bf16)

    def gw_copy(step, dest, source):
        return remote(gw_out.at[step], gw_in.at[source], gw_send.at[step], gw_recv.at[step], (dest, dp_me))

    def gf_copy(step, dest, source):
        return remote(gf_out.at[dest], gf_in.at[source], gf_send.at[step], gf_recv.at[step], (dest, dp_me))

    def ahead(step):
        return lax.rem(me + step, seq_count)

    def behind(step):
        return lax.rem(me + seq_count - step, seq_count)

    for step in range(1, seq_count):
        dest = ahead(step)
        gw_out[step] = weight_piece(dest)
        gw_copy(step, dest, me).start()
    gw_in[me] = weight_piece(me)

    low_at = lax.broadcasted_iota(jnp.int32, (8, span), 0)
    for filt in range(group_filters):
        cols = filt_cols(filt)
        grads = jnp.concatenate([grad_win[part, :, cols] for part in range(LEVEL)], 1)
        for lag in range(blocks):
            inputs = jnp.concatenate([prod_win[own_slot + part - lag, :, cols] for part in range(LEVEL)], 1)
            lags[:, lag * rows : (lag + 1) * rows] = lax.dot_general(
                inputs, grads, (((1,), (1,)), ((), ())), preferred_element_type=f32)
        height = rows // 2
        total = lags[:height] + pltpu.roll(lags[height:], span - height, 1)
        while height > 8:
            height //= 2
            total = total[:height] + pltpu.roll(total[height:], span - height, 1)
        for bit in (1, 2, 4):
            total = jnp.where((low_at & bit) != 0, pltpu.roll(total, span - bit, 1), total)
        sums = jnp.sum(total, axis=0, keepdims=True)
        for dest in range(seq_count):
            gf_out[dest, filt : filt + 1, :] = sums[:, dest * tap_piece : (dest + 1) * tap_piece]
    for step in range(1, seq_count):
        gf_copy(step, ahead(step), me).start()
    gf_in[me] = gf_out[me]

    for offset in range(LEVEL):
        @pl.when(grad_takes(reach - 1))
        def _():
            grad_hop(reach - 1, offset).wait_recv()
    for offset in (2, 3, 1, 0):
        part = peers[offset]
        grad = jnp.concatenate(
            [jnp.dot(band_back[filt],
                     grad_win[pl.ds(part, blocks), :, filt_cols(filt)].reshape(span, group_width),
                     preferred_element_type=f32) for filt in range(group_filters)], 1).astype(bf16)
        if offset:
            gp_out[part] = grad
            copy = remote(gp_out.at[part], gp_in.at[rank], gp_sem.at[0, offset], gp_sem.at[1, offset], ids[offset])
            copy.start()
            gp_copies.append(copy)
        else:
            gp_in[part] = grad

    for offset in range(1, LEVEL):
        remote(gq_out.at[peers[offset]], gq_in.at[peers[offset]],
               gq_sem.at[0, offset], gq_sem.at[1, offset], ids[offset]).wait_recv()
    for part in range(LEVEL):
        gquery_ref[:, part * chan : (part + 1) * chan] = gq_in[part]
    for step in range(1, seq_count):
        gw_copy(step, ahead(step), behind(step)).wait_recv()
        gf_copy(step, ahead(step), behind(step)).wait_recv()
    for part in range(LEVEL):
        total = gw_in[part].astype(f32)
        taps_total = gf_in[part, :group_filters, :]
        for other in range(1, level_count):
            total += gw_in[other * LEVEL + part].astype(f32)
            taps_total += gf_in[other * LEVEL + part, :group_filters, :]
        gweight_ref[part * chan : (part + 1) * chan, :] = total
        gfilters_ref[part * group_filters : (part + 1) * group_filters, :] = taps_total
    for offset in range(1, LEVEL):
        remote(gp_out.at[peers[offset]], gp_in.at[peers[offset]],
               gp_sem.at[0, offset], gp_sem.at[1, offset], ids[offset]).wait_recv()
    for part in range(LEVEL):
        cols = slice(part * chan, (part + 1) * chan)
        grad = gp_in[part].astype(f32)
        gkey_ref[:, cols] = (grad * value_ref[:, cols].astype(f32)).astype(bf16)
        gvalue_ref[:, cols] = (grad * key_ref[:, cols].astype(f32)).astype(bf16)

    for copy in [taps_copy] + prod_copies + query_copies + mixed_copies + gq_copies + gp_copies:
        copy.wait_send()
    for hop in range(reach):
        for offset in range(LEVEL):
            @pl.when(prod_sends(hop))
            def _():
                prod_hop(hop, offset).wait_send()

            @pl.when(grad_sends(hop))
            def _():
                grad_hop(hop, offset).wait_send()
    for step in range(1, seq_count):
        gw_copy(step, ahead(step), me).wait_send()
        gf_copy(step, ahead(step), me).wait_send()


def per_device_fused(query_in, key_in, value_in, filters, out_weight, grad_mixed):
    f32, bf16 = jnp.float32, jnp.bfloat16
    rows, width = query_in.shape
    seq_count, dp_count = lax.axis_size("seq"), lax.axis_size("dp")
    total_cols = width * dp_count
    filter_len = filters.shape[1] * dp_count
    local_filters = NUM_FILTERS // dp_count
    group_filters = local_filters // LEVEL
    chan = width // LEVEL
    reach = filter_len // (rows * LEVEL)
    span = filter_len + rows
    slots = (reach + 1) * LEVEL
    piece, tap_piece = total_cols // seq_count, filter_len // seq_count
    vmem = pl.BlockSpec(memory_space=pltpu.VMEM)
    dma = pltpu.SemaphoreType.DMA
    sub = -(-group_filters // 8) * 8
    return pl.pallas_call(
        fused_kernel,
        out_shape=(
            jax.ShapeDtypeStruct((rows, width), bf16),
            jax.ShapeDtypeStruct((rows, width), bf16),
            jax.ShapeDtypeStruct((rows, width), bf16),
            jax.ShapeDtypeStruct((width, piece), f32),
            jax.ShapeDtypeStruct((local_filters, tap_piece), f32),
        ),
        in_specs=[vmem, vmem, vmem, vmem, pl.BlockSpec(memory_space=pl.ANY), vmem],
        out_specs=(vmem,) * 5,
        scratch_shapes=[
            pltpu.VMEM((dp_count,) + filters.shape, bf16),
            pltpu.VMEM((dp_count, LEVEL * rows, width), bf16),
            pltpu.VMEM((chan, total_cols), bf16),
            pltpu.VMEM((LEVEL, rows, chan), bf16),
            pltpu.VMEM((slots, rows, chan), bf16),
            pltpu.VMEM((slots, rows, chan), bf16),
            pltpu.VMEM((LEVEL, rows, chan), bf16),
            pltpu.VMEM((chan, LEVEL * rows), bf16),
            pltpu.VMEM((LEVEL, rows, chan), f32),
            pltpu.VMEM((group_filters, rows, span), bf16),
            pltpu.VMEM((group_filters, rows, span), bf16),
            pltpu.VMEM((rows, span), f32),
            pltpu.VMEM((LEVEL, rows, chan), bf16),
            pltpu.VMEM((LEVEL, rows, chan), bf16),
            pltpu.VMEM((LEVEL, rows, chan), bf16),
            pltpu.VMEM((LEVEL, rows, chan), bf16),
            pltpu.VMEM((seq_count, chan, piece), bf16),
            pltpu.VMEM((seq_count, chan, piece), bf16),
            pltpu.VMEM((seq_count, sub, tap_piece), f32),
            pltpu.VMEM((seq_count, sub, tap_piece), f32),
            dma, dma((2,)), dma((2, LEVEL)), dma((2, LEVEL)), dma((2, 7)),
            dma((reach, LEVEL)), dma((reach, LEVEL)), dma((reach, LEVEL)), dma((reach, LEVEL)),
            dma((2, LEVEL)), dma((2, LEVEL)),
            dma((seq_count,)), dma((seq_count,)), dma((seq_count,)), dma((seq_count,)),
        ],
        compiler_params=pltpu.CompilerParams(
            collective_id=0, has_side_effects=True, vmem_limit_bytes=56 * 1024 * 1024),
    )(query_in, key_in, value_in, filters, out_weight, grad_mixed)


def fits_fused(query_in, filters, seq_count, dp_count):
    rows, width = query_in.shape[0] // seq_count, query_in.shape[1] // dp_count
    filter_len = filters.shape[1]
    return (
        dp_count == 2
        and seq_count % LEVEL == 0
        and NUM_FILTERS % (dp_count * LEVEL) == 0
        and filter_len % (rows * LEVEL) == 0
        and rows % 128 == 0
        and rows & (rows - 1) == 0
        and width % (NUM_FILTERS // dp_count * 128) == 0
        and filter_len % (seq_count * 128) == 0
        and width % (width * dp_count // seq_count) == 0
        and (width * dp_count) % (seq_count * 128) == 0
    )


def solution(mesh):
    in_specs = (
        P("seq", "dp"),
        P("seq", "dp"),
        P("seq", "dp"),
        P(None, "dp"),
        P("dp", None),
        P("seq", "dp"),
    )
    out_specs = (P("seq", "dp"), P("seq", "dp"), P("seq", "dp"), P("dp", "seq"), P("dp", "seq"))
    seq_count, dp_count = mesh.shape["seq"], mesh.shape["dp"]

    def whole(query_in, key_in, value_in, filters, out_weight, grad_mixed):
        fused = fits_fused(query_in, filters, seq_count, dp_count)
        return jax.shard_map(
            per_device_fused if fused else per_device,
            mesh=mesh, in_specs=in_specs, out_specs=out_specs, check_vma=False,
        )(query_in, key_in, value_in, filters, out_weight, grad_mixed)

    return whole
```

```python
import jax
import jax.numpy as jnp
from jax import lax
from jax.experimental import pallas as pl
from jax.experimental.pallas import tpu as pltpu
from jax.sharding import PartitionSpec as P

NUM_FILTERS = 16


def from_behind(block, axis, distance):
    devices = range(lax.axis_size(axis))
    route = [(i - distance, i) for i in devices if i - distance in devices]
    return lax.ppermute(block, axis, route)


def band_matrix(vector, row_count, col_count):
    period = vector.shape[0]
    tiled = jnp.tile(vector, (row_count,))[: row_count * (period - 1)]
    return tiled.reshape(row_count, period - 1)[:, :col_count]


def input_doubling(own_shard, reach_count):
    window = own_shard
    covered = 1
    for bit_index in range(reach_count.bit_length() - 1):
        window = jnp.concatenate([from_behind(window, "seq", covered), window], 0)
        covered = covered * 2
    farthest = from_behind(own_shard, "seq", reach_count)
    return jnp.concatenate([farthest, window], 0)


def grad_doubling(own_shard, reach_count):
    window = own_shard
    covered = 1
    for bit_index in range(reach_count.bit_length() - 1):
        window = jnp.concatenate([window, from_behind(window, "seq", -covered)], 0)
        covered = covered * 2
    farthest = from_behind(own_shard, "seq", -reach_count)
    return jnp.concatenate([window, farthest], 0)


def per_device(query_in, key_in, value_in, filters, out_weight, grad_mixed):
    tok_rows, local_width = query_in.shape
    dp_count = lax.axis_size("dp")
    filter_len = filters.shape[1] * dp_count
    local_filters = NUM_FILTERS // dp_count
    group_width = local_width // local_filters
    reach_count = filter_len // tok_rows
    span_rows = filter_len + tok_rows
    period = span_rows + tok_rows
    all_taps = lax.all_gather(filters, "dp", axis=1, tiled=True)
    owned_taps = lax.dynamic_slice_in_dim(
        all_taps, lax.axis_index("dp") * local_filters, local_filters, 0
    )
    products = (key_in.astype(jnp.float32) * value_in.astype(jnp.float32)).astype(jnp.bfloat16)
    window_in = input_doubling(products, reach_count)
    head_zeros = jnp.zeros((local_filters, 1), jnp.bfloat16)
    tail_zeros = jnp.zeros((local_filters, period - 1 - filter_len), jnp.bfloat16)
    forward_vectors = jnp.concatenate([head_zeros, owned_taps[:, ::-1], tail_zeros], 1)
    after_zeros = jnp.zeros((local_filters, period - filter_len), jnp.bfloat16)
    backward_vectors = jnp.concatenate([owned_taps, after_zeros], 1)
    conv_parts = []
    for group_index in range(local_filters):
        forward_band = band_matrix(forward_vectors[group_index], tok_rows, span_rows)
        window_part = window_in[:, group_index * group_width : (group_index + 1) * group_width]
        conv_parts.append(jnp.dot(forward_band, window_part, preferred_element_type=jnp.float32))
    conv_out = jnp.concatenate(conv_parts, 1)
    gated = (query_in.astype(jnp.float32) * conv_out).astype(jnp.bfloat16)
    block_in = lax.all_gather(grad_mixed, "dp", axis=1, tiled=True)
    grad_part = lax.dot_general(
        block_in, out_weight, (((1,), (1,)), ((), ())), preferred_element_type=jnp.float32
    )
    block_grad = lax.dot_general(
        gated, block_in, (((0,), (0,)), ((), ())), preferred_element_type=jnp.float32
    )
    grad_query = (grad_part * conv_out).astype(jnp.bfloat16)
    grad_conv = (grad_part * query_in.astype(jnp.float32)).astype(jnp.bfloat16)
    window_grad = grad_doubling(grad_conv, reach_count)
    grad_parts = []
    filter_rows = []
    for group_index in range(local_filters):
        low_col = group_index * group_width
        backward_band = band_matrix(backward_vectors[group_index], tok_rows, span_rows)
        grad_window = window_grad[:, low_col : low_col + group_width]
        grad_parts.append(jnp.dot(backward_band, grad_window, preferred_element_type=jnp.float32))
        own_grads = grad_conv[:, low_col : low_col + group_width]
        window_part = window_in[:, low_col : low_col + group_width]
        lagged = lax.dot_general(
            own_grads, window_part, (((1,), (1,)), ((), ())), preferred_element_type=jnp.float32
        )
        flattened = jnp.pad(lagged.reshape(tok_rows * span_rows), (0, tok_rows))
        skewed = flattened.reshape(tok_rows, span_rows + 1)
        diagonal_sums = jnp.sum(skewed, axis=0)
        filter_rows.append(diagonal_sums[1 : filter_len + 1][::-1])
    grad_products = jnp.concatenate(grad_parts, 1)
    grad_key = (grad_products * value_in.astype(jnp.float32)).astype(jnp.bfloat16)
    grad_value = (grad_products * key_in.astype(jnp.float32)).astype(jnp.bfloat16)
    filter_grad = jnp.stack(filter_rows, 0)
    grad_weight, grad_filters = (
        lax.psum_scatter(block_grad, "seq", scatter_dimension=1, tiled=True),
        lax.psum_scatter(filter_grad, "seq", scatter_dimension=1, tiled=True),
    )
    return (grad_query, grad_key, grad_value, grad_weight, grad_filters)


MIXED_CHUNKS = 4
LEVEL = 4


def transposed(block):
    return block.astype(jnp.float32).T.astype(jnp.bfloat16)


def fused_kernel(
    query_ref, key_ref, value_ref, taps_ref, weight_ref, mixed_ref,
    gquery_ref, gprod_ref, gweight_ref, gfilters_ref,
    taps_all, mixed_all, weight_own, prod_out, prod_win, grad_win, query_lvl, gated_lvl,
    part_lvl, band_back, band_fwd, lags, gq_out, gq_in, gp_out, gp_in,
    gw_out, gw_in, ch_out, ch_in, ch_sum, gf_out, gf_in,
    weight_sem, taps_sem, prod_sem, query_sem, mixed_sem, xz_send, xz_recv, gz_send, gz_recv,
    gq_sem, gp_sem, gw_send, gw_recv, ch_send, ch_recv, gf_send, gf_recv,
):
    f32, bf16 = jnp.float32, jnp.bfloat16
    seq_count = lax.axis_size("seq")
    me, dp_me = lax.axis_index("seq"), lax.axis_index("dp")
    level_count = seq_count // LEVEL
    level, rank = me // LEVEL, lax.rem(me, LEVEL)
    base = level * LEVEL
    rows, width = query_ref.shape
    chan = width // LEVEL
    group_filters = band_back.shape[0]
    group_width = chan // group_filters
    span = band_back.shape[2]
    blocks = span // rows
    reach = (blocks - 1) // LEVEL
    local_filters = group_filters * LEVEL
    piece = gweight_ref.shape[1]
    tap_piece = gfilters_ref.shape[1]

    def flip(index, offset):
        low, high = lax.rem(index, 2), index // 2
        if offset & 1:
            low = 1 - low
        if offset & 2:
            high = 1 - high
        return high * 2 + low

    peers = [flip(rank, offset) for offset in range(LEVEL)]
    ids = [(base + peer, dp_me) for peer in peers]
    across = (me, 1 - dp_me)

    def remote(src, dst, send, recv, device):
        return pltpu.make_async_remote_copy(
            src_ref=src, dst_ref=dst, send_sem=send, recv_sem=recv, device_id=device,
            device_id_type=pl.DeviceIdType.MESH)

    barrier = pltpu.get_barrier_semaphore()
    for step in range(1, seq_count):
        pl.semaphore_signal(barrier, inc=1, device_id=(lax.rem(me + step, seq_count), dp_me),
                            device_id_type=pl.DeviceIdType.MESH)
    pl.semaphore_signal(barrier, inc=1, device_id=across, device_id_type=pl.DeviceIdType.MESH)

    weight_copy = pltpu.make_async_copy(
        weight_ref.at[pl.ds(pl.multiple_of(rank * chan, chan), chan), :], weight_own, weight_sem)
    weight_copy.start()
    for part in range(LEVEL):
        cols = slice(part * chan, (part + 1) * chan)
        prod_out[part] = (key_ref[:, cols].astype(f32) * value_ref[:, cols].astype(f32)).astype(bf16)
    own_slot = reach * LEVEL

    def token_rows(part):
        return pl.ds(pl.multiple_of(part * rows, rows), rows)

    def chan_cols(part):
        return pl.ds(pl.multiple_of(part * chan, chan), chan)

    pl.semaphore_wait(barrier, seq_count)

    taps_copy = remote(taps_ref, taps_all.at[dp_me], taps_sem.at[0], taps_sem.at[1], across)
    taps_copy.start()
    prod_copies, query_copies = [], []
    for offset in range(1, LEVEL):
        copy = remote(prod_out.at[peers[offset]], prod_win.at[own_slot + rank],
                      prod_sem.at[0, offset], prod_sem.at[1, offset], ids[offset])
        copy.start()
        prod_copies.append(copy)

    def mixed_copy(sem, src, dp_at, part, device):
        dst = mixed_all.at[dp_at, token_rows(part), :]
        return remote(dst if src is None else src, dst, mixed_sem.at[0, sem], mixed_sem.at[1, sem], device)

    chunk_rows = rows // MIXED_CHUNKS

    def mixed_chunk(sem, chunk, src, dp_at, part, device):
        start = pl.multiple_of(part * rows + chunk * chunk_rows, chunk_rows)
        dst = mixed_all.at[dp_at, pl.ds(start, chunk_rows), :]
        source = dst if src is None else src.at[pl.ds(chunk * chunk_rows, chunk_rows), :]
        at = 7 + (MIXED_CHUNKS if sem else 0) + chunk
        return remote(source, dst, mixed_sem.at[0, at], mixed_sem.at[1, at], device)

    mixed_copies = [mixed_chunk(0, chunk, mixed_ref, dp_me, rank, ids[2]) for chunk in range(MIXED_CHUNKS)] + [
        mixed_copy(1, mixed_ref, dp_me, rank, across),
        mixed_copy(2, mixed_ref, dp_me, rank, ids[1]),
    ]
    for copy in mixed_copies:
        copy.start()
    for offset in range(1, LEVEL):
        copy = remote(query_ref.at[:, chan_cols(peers[offset])], query_lvl.at[rank],
                      query_sem.at[0, offset], query_sem.at[1, offset], ids[offset])
        copy.start()
        query_copies.append(copy)

    prod_win[own_slot + rank] = prod_out[rank]
    query_lvl[rank] = query_ref[:, chan_cols(rank)]
    mixed_all[dp_me, token_rows(rank), :] = mixed_ref[...]
    taps_all[dp_me] = taps_ref[...]

    for hop in range(reach):
        @pl.when(level <= hop)
        def _():
            for part in range(LEVEL):
                prod_win[(reach - 1 - hop) * LEVEL + part] = jnp.zeros((rows, chan), bf16)

        @pl.when(level + hop + 1 >= level_count)
        def _():
            for part in range(LEVEL):
                grad_win[(hop + 1) * LEVEL + part] = jnp.zeros((rows, chan), bf16)

    def prod_hop(hop, offset):
        part = peers[offset]
        return remote(prod_win.at[(reach - hop) * LEVEL + part], prod_win.at[(reach - hop - 1) * LEVEL + part],
                      xz_send.at[hop, offset], xz_recv.at[hop, offset],
                      (lax.rem(me + LEVEL, seq_count), dp_me))

    def grad_hop(hop, offset):
        part = peers[offset]
        return remote(grad_win.at[hop * LEVEL + part], grad_win.at[(hop + 1) * LEVEL + part],
                      gz_send.at[hop, offset], gz_recv.at[hop, offset],
                      (lax.rem(me + seq_count - LEVEL, seq_count), dp_me))

    def prod_sends(hop):
        return (level >= hop) & (level < level_count - 1)

    def prod_takes(hop):
        return level >= hop + 1

    def grad_sends(hop):
        return (level + hop < level_count) & (level > 0)

    def grad_takes(hop):
        return level + hop + 1 < level_count

    for offset in range(LEVEL):
        if offset:
            wait_in = remote(prod_out.at[peers[offset]], prod_win.at[own_slot + peers[offset]],
                             prod_sem.at[0, offset], prod_sem.at[1, offset], ids[offset])
            wait_in.wait_recv()

        @pl.when(prod_sends(0))
        def _():
            prod_hop(0, offset).start()

    remote(taps_ref, taps_all.at[1 - dp_me], taps_sem.at[0], taps_sem.at[1], across).wait_recv()
    halves = taps_all.shape[0]
    row_at = lax.broadcasted_iota(jnp.int32, taps_all.shape[1:], 0)
    sub_at = lax.broadcasted_iota(jnp.int32, (8, span + rows), 0)
    for filt in range(group_filters):
        wanted = dp_me * local_filters + rank * group_filters + filt
        taps_row = jnp.concatenate(
            [jnp.sum(jnp.where(row_at == wanted, taps_all[half].astype(f32), 0.0), axis=0, keepdims=True)
             for half in range(halves)] + [jnp.zeros((1, 2 * rows), f32)], 1)
        band = jnp.broadcast_to(taps_row, (8, span + rows))
        for bit in (1, 2, 4):
            band = jnp.where((sub_at & bit) != 0, pltpu.roll(band, bit, 1), band)
        height = 8
        while height < rows:
            band = jnp.concatenate([band, pltpu.roll(band, height, 1)], 0)
            height *= 2
        for lag in range(blocks):
            tile = band[:, lag * rows : (lag + 1) * rows]
            band_back[filt, :, lag * rows : (lag + 1) * rows] = tile.astype(bf16)
            at = (blocks - 1 - lag) * rows
            band_fwd[filt, :, at : at + rows] = tile.T.astype(bf16)

    def mixed_wait(sem, dp_at, part):
        mixed_copy(sem, None, dp_at, part, across).wait_recv()

    mixed_wait(1, 1 - dp_me, rank)
    relay = mixed_copy(3, None, 1 - dp_me, rank, ids[1])
    relay.start()
    mixed_copies.append(relay)
    for chunk in range(MIXED_CHUNKS):
        mixed_chunk(0, chunk, None, dp_me, peers[2], across).wait_recv()
        relay = mixed_chunk(4, chunk, None, dp_me, peers[2], across)
        relay.start()
        mixed_copies.append(relay)
    relay = mixed_copy(5, None, dp_me, peers[2], ids[1])
    relay.start()
    mixed_copies.append(relay)
    mixed_wait(2, dp_me, peers[1])
    mixed_wait(3, 1 - dp_me, peers[1])
    mixed_wait(5, dp_me, peers[3])
    weight_copy.wait()

    def level_grad(offset):
        part = peers[offset]
        total = jnp.zeros((rows, chan), f32)
        for half in range(halves):
            total += lax.dot_general(
                mixed_all[half, token_rows(part), :], weight_own[:, half * width : (half + 1) * width],
                (((1,), (1,)), ((), ())), preferred_element_type=f32)
        part_lvl[part] = total
        if offset:
            remote(query_ref.at[:, chan_cols(peers[offset])], query_lvl.at[part],
                   query_sem.at[0, offset], query_sem.at[1, offset], ids[offset]).wait_recv()
        grad_win[part] = (total * query_lvl[part].astype(f32)).astype(bf16)

        @pl.when(grad_sends(0))
        def _():
            grad_hop(0, offset).start()

    level_grad(0)
    level_grad(1)
    for hop in range(1, reach):
        for offset in range(LEVEL):
            @pl.when(prod_takes(hop - 1))
            def _():
                prod_hop(hop - 1, offset).wait_recv()

            @pl.when(prod_sends(hop))
            def _():
                prod_hop(hop, offset).start()
    for chunk in range(MIXED_CHUNKS):
        mixed_chunk(4, chunk, None, 1 - dp_me, peers[2], across).wait_recv()
    relay = mixed_copy(6, None, 1 - dp_me, peers[2], ids[1])
    relay.start()
    mixed_copies.append(relay)
    level_grad(2)
    mixed_wait(6, 1 - dp_me, peers[3])
    level_grad(3)

    for offset in range(LEVEL):
        @pl.when(prod_takes(reach - 1))
        def _():
            prod_hop(reach - 1, offset).wait_recv()

    def filt_cols(filt):
        return slice(filt * group_width, (filt + 1) * group_width)

    gq_copies, gp_copies = [], []
    for offset in (1, 2, 3, 0):
        part = peers[offset]
        conv = jnp.concatenate(
            [jnp.dot(band_fwd[filt],
                     prod_win[pl.ds(part, blocks), :, filt_cols(filt)].reshape(span, group_width),
                     preferred_element_type=f32) for filt in range(group_filters)], 1)
        gated = (query_lvl[part].astype(f32) * conv).astype(bf16)
        gated_lvl[:, token_rows(part)] = transposed(gated)
        grad = (part_lvl[part] * conv).astype(bf16)
        if offset:
            gq_out[part] = grad
            copy = remote(gq_out.at[part], gq_in.at[rank], gq_sem.at[0, offset], gq_sem.at[1, offset], ids[offset])
            copy.start()
            gq_copies.append(copy)
        else:
            gq_in[part] = grad

    for hop in range(1, reach):
        for offset in range(LEVEL):
            @pl.when(grad_takes(hop - 1))
            def _():
                grad_hop(hop - 1, offset).wait_recv()

            @pl.when(grad_sends(hop))
            def _():
                grad_hop(hop, offset).start()

    level_cols = piece * LEVEL
    per_half = width // level_cols

    def weight_part(owner):
        cols = pl.ds(pl.multiple_of(lax.rem(owner, per_half) * level_cols, level_cols), level_cols)
        return jnp.dot(gated_lvl[...], mixed_all[owner // per_half, :, cols], preferred_element_type=f32)

    def chain_copy(way, distance):
        step = LEVEL if way == 0 else seq_count - LEVEL
        return remote(ch_out.at[way, distance], ch_in.at[way, distance], ch_send.at[way, distance],
                      ch_recv.at[way, distance], (lax.rem(me + step, seq_count), dp_me))

    def chain_sends(way, distance):
        return level + distance < level_count if way == 0 else level >= distance

    def chain_takes(way, distance):
        if way == 0:
            return (level >= 1) & (level - 1 + distance < level_count)
        return (level + 1 < level_count) & (level + 1 >= distance)

    def gf_copy(step, dest, source):
        return remote(gf_out.at[dest], gf_in.at[source], gf_send.at[step], gf_recv.at[step], (dest, dp_me))

    def ahead(step):
        return lax.rem(me + step, seq_count)

    def behind(step):
        return lax.rem(me + seq_count - step, seq_count)

    for distance in range(level_count - 1, 0, -1):
        for way in (0, 1):
            @pl.when(chain_sends(way, distance))
            def _():
                if distance + 1 < level_count:
                    @pl.when(chain_takes(way, distance + 1))
                    def _():
                        chain_copy(way, distance + 1).wait_recv()
                        ch_sum[...] = ch_in[way, distance + 1].astype(f32)

                    @pl.when(jnp.logical_not(chain_takes(way, distance + 1)))
                    def _():
                        ch_sum[...] = jnp.zeros_like(ch_sum)
                    total = ch_sum[...] + weight_part(level + distance if way == 0 else level - distance)
                else:
                    total = weight_part(level + distance if way == 0 else level - distance)
                ch_out[way, distance] = total.astype(bf16)
                chain_copy(way, distance).start()

    low_at = lax.broadcasted_iota(jnp.int32, (8, span), 0)
    for filt in range(group_filters):
        cols = filt_cols(filt)
        grads = jnp.concatenate([grad_win[part, :, cols] for part in range(LEVEL)], 1)
        for lag in range(blocks):
            inputs = jnp.concatenate([prod_win[own_slot + part - lag, :, cols] for part in range(LEVEL)], 1)
            lags[:, lag * rows : (lag + 1) * rows] = lax.dot_general(
                inputs, grads, (((1,), (1,)), ((), ())), preferred_element_type=f32)
        height = rows // 2
        total = lags[:height] + pltpu.roll(lags[height:], span - height, 1)
        while height > 8:
            height //= 2
            total = total[:height] + pltpu.roll(total[height:], span - height, 1)
        for bit in (1, 2, 4):
            total = jnp.where((low_at & bit) != 0, pltpu.roll(total, span - bit, 1), total)
        sums = jnp.sum(total, axis=0, keepdims=True)
        for dest in range(seq_count):
            gf_out[dest, filt : filt + 1, :] = sums[:, dest * tap_piece : (dest + 1) * tap_piece]
    for step in range(1, seq_count):
        gf_copy(step, ahead(step), me).start()
    gf_in[me] = gf_out[me]

    for offset in range(LEVEL):
        @pl.when(grad_takes(reach - 1))
        def _():
            grad_hop(reach - 1, offset).wait_recv()
    for offset in (2, 3, 1, 0):
        part = peers[offset]
        grad = jnp.concatenate(
            [jnp.dot(band_back[filt],
                     grad_win[pl.ds(part, blocks), :, filt_cols(filt)].reshape(span, group_width),
                     preferred_element_type=f32) for filt in range(group_filters)], 1).astype(bf16)
        if offset:
            gp_out[part] = grad
            copy = remote(gp_out.at[part], gp_in.at[rank], gp_sem.at[0, offset], gp_sem.at[1, offset], ids[offset])
            copy.start()
            gp_copies.append(copy)
        else:
            gp_in[part] = grad

    ch_sum[...] = weight_part(level)
    for way in (0, 1):
        @pl.when(chain_takes(way, 1))
        def _():
            chain_copy(way, 1).wait_recv()
            ch_sum[...] += ch_in[way, 1].astype(f32)

    def gw_copy(offset, slot):
        return remote(gw_out.at[peers[offset]], gw_in.at[slot], gw_send.at[offset], gw_recv.at[offset], ids[offset])

    for part in range(LEVEL):
        gw_out[part] = ch_sum[:, part * piece : (part + 1) * piece].astype(bf16)
    for offset in range(1, LEVEL):
        gw_copy(offset, rank).start()
    gw_in[rank] = gw_out[rank]

    for offset in range(1, LEVEL):
        remote(gq_out.at[peers[offset]], gq_in.at[peers[offset]],
               gq_sem.at[0, offset], gq_sem.at[1, offset], ids[offset]).wait_recv()
    for part in range(LEVEL):
        gquery_ref[:, part * chan : (part + 1) * chan] = gq_in[part]
    for step in range(1, seq_count):
        gf_copy(step, ahead(step), behind(step)).wait_recv()
    for part in range(LEVEL):
        taps_total = gf_in[part, :group_filters, :]
        for other in range(1, level_count):
            taps_total += gf_in[other * LEVEL + part, :group_filters, :]
        gfilters_ref[part * group_filters : (part + 1) * group_filters, :] = taps_total
    for offset in range(1, LEVEL):
        remote(gp_out.at[peers[offset]], gp_in.at[peers[offset]],
               gp_sem.at[0, offset], gp_sem.at[1, offset], ids[offset]).wait_recv()
    for offset in range(1, LEVEL):
        gw_copy(offset, peers[offset]).wait_recv()
    for part in range(LEVEL):
        gweight_ref[part * chan : (part + 1) * chan, :] = gw_in[part].astype(f32)
    for part in range(LEVEL):
        cols = slice(part * chan, (part + 1) * chan)
        gprod_ref[:, cols] = gp_in[part]

    for copy in [taps_copy] + prod_copies + query_copies + mixed_copies + gq_copies + gp_copies:
        copy.wait_send()
    for hop in range(reach):
        for offset in range(LEVEL):
            @pl.when(prod_sends(hop))
            def _():
                prod_hop(hop, offset).wait_send()

            @pl.when(grad_sends(hop))
            def _():
                grad_hop(hop, offset).wait_send()
    for offset in range(1, LEVEL):
        gw_copy(offset, rank).wait_send()
    for distance in range(1, level_count):
        for way in (0, 1):
            @pl.when(chain_sends(way, distance))
            def _():
                chain_copy(way, distance).wait_send()
    for step in range(1, seq_count):
        gf_copy(step, ahead(step), me).wait_send()


def per_device_fused(query_in, key_in, value_in, filters, out_weight, grad_mixed):
    f32, bf16 = jnp.float32, jnp.bfloat16
    rows, width = query_in.shape
    seq_count, dp_count = lax.axis_size("seq"), lax.axis_size("dp")
    total_cols = width * dp_count
    filter_len = filters.shape[1] * dp_count
    local_filters = NUM_FILTERS // dp_count
    group_filters = local_filters // LEVEL
    chan = width // LEVEL
    reach = filter_len // (rows * LEVEL)
    span = filter_len + rows
    slots = (reach + 1) * LEVEL
    level_count = seq_count // LEVEL
    piece, tap_piece = total_cols // seq_count, filter_len // seq_count
    vmem = pl.BlockSpec(memory_space=pltpu.VMEM)
    dma = pltpu.SemaphoreType.DMA
    sub = -(-group_filters // 8) * 8
    grad_query, grad_products, grad_weight, grad_filters = pl.pallas_call(
        fused_kernel,
        out_shape=(
            jax.ShapeDtypeStruct((rows, width), bf16),
            jax.ShapeDtypeStruct((rows, width), bf16),
            jax.ShapeDtypeStruct((width, piece), f32),
            jax.ShapeDtypeStruct((local_filters, tap_piece), f32),
        ),
        in_specs=[vmem, vmem, vmem, vmem, pl.BlockSpec(memory_space=pl.ANY), vmem],
        out_specs=(vmem,) * 4,
        scratch_shapes=[
            pltpu.VMEM((dp_count,) + filters.shape, bf16),
            pltpu.VMEM((dp_count, LEVEL * rows, width), bf16),
            pltpu.VMEM((chan, total_cols), bf16),
            pltpu.VMEM((LEVEL, rows, chan), bf16),
            pltpu.VMEM((slots, rows, chan), bf16),
            pltpu.VMEM((slots, rows, chan), bf16),
            pltpu.VMEM((LEVEL, rows, chan), bf16),
            pltpu.VMEM((chan, LEVEL * rows), bf16),
            pltpu.VMEM((LEVEL, rows, chan), f32),
            pltpu.VMEM((group_filters, rows, span), bf16),
            pltpu.VMEM((group_filters, rows, span), bf16),
            pltpu.VMEM((rows, span), f32),
            pltpu.VMEM((LEVEL, rows, chan), bf16),
            pltpu.VMEM((LEVEL, rows, chan), bf16),
            pltpu.VMEM((LEVEL, rows, chan), bf16),
            pltpu.VMEM((LEVEL, rows, chan), bf16),
            pltpu.VMEM((LEVEL, chan, piece), bf16),
            pltpu.VMEM((LEVEL, chan, piece), bf16),
            pltpu.VMEM((2, level_count, chan, piece * LEVEL), bf16),
            pltpu.VMEM((2, level_count, chan, piece * LEVEL), bf16),
            pltpu.VMEM((chan, piece * LEVEL), f32),
            pltpu.VMEM((seq_count, sub, tap_piece), f32),
            pltpu.VMEM((seq_count, sub, tap_piece), f32),
            dma, dma((2,)), dma((2, LEVEL)), dma((2, LEVEL)), dma((2, 7 + 2 * MIXED_CHUNKS)),
            dma((reach, LEVEL)), dma((reach, LEVEL)), dma((reach, LEVEL)), dma((reach, LEVEL)),
            dma((2, LEVEL)), dma((2, LEVEL)),
            dma((LEVEL,)), dma((LEVEL,)), dma((2, level_count)), dma((2, level_count)),
            dma((seq_count,)), dma((seq_count,)),
        ],
        compiler_params=pltpu.CompilerParams(
            collective_id=0, has_side_effects=True, vmem_limit_bytes=56 * 1024 * 1024),
    )(query_in, key_in, value_in, filters, out_weight, grad_mixed)
    grad_key = (grad_products.astype(f32) * value_in.astype(f32)).astype(bf16)
    grad_value = (grad_products.astype(f32) * key_in.astype(f32)).astype(bf16)
    return grad_query, grad_key, grad_value, grad_weight, grad_filters


def fits_fused(query_in, filters, seq_count, dp_count):
    rows, width = query_in.shape[0] // seq_count, query_in.shape[1] // dp_count
    filter_len = filters.shape[1]
    return (
        dp_count == 2
        and seq_count % LEVEL == 0
        and NUM_FILTERS % (dp_count * LEVEL) == 0
        and filter_len % (rows * LEVEL) == 0
        and rows % 128 == 0
        and rows & (rows - 1) == 0
        and width % (NUM_FILTERS // dp_count * 128) == 0
        and filter_len % (seq_count * 128) == 0
        and width % (width * dp_count // seq_count * LEVEL) == 0
        and rows % (16 * MIXED_CHUNKS) == 0
        and (width * dp_count) % (seq_count * 128) == 0
    )


def solution(mesh):
    in_specs = (
        P("seq", "dp"),
        P("seq", "dp"),
        P("seq", "dp"),
        P(None, "dp"),
        P("dp", None),
        P("seq", "dp"),
    )
    out_specs = (P("seq", "dp"), P("seq", "dp"), P("seq", "dp"), P("dp", "seq"), P("dp", "seq"))
    seq_count, dp_count = mesh.shape["seq"], mesh.shape["dp"]

    def whole(query_in, key_in, value_in, filters, out_weight, grad_mixed):
        fused = fits_fused(query_in, filters, seq_count, dp_count)
        return jax.shard_map(
            per_device_fused if fused else per_device,
            mesh=mesh, in_specs=in_specs, out_specs=out_specs, check_vma=False,
        )(query_in, key_in, value_in, filters, out_weight, grad_mixed)

    return whole
```
